32 devices in a mesh: tile: 8 (over y, x, core), slab: 4 (over z).
Axes of the slice: x: 2, y: 2, z: 4, core: 2. Of those that a mesh axis runs over, the one named last changes fastest.
Arguments:
- stored: float32 [32, 8, 256, 1024], P('tile', 'slab'), may hold values from -6 to 6
- offsets: int32 [2, 2, 32], P(None, None, ('tile', 'slab')), may hold values from 0 to 128
Outputs:
- surface: float32 [2, 32, 128, 1024], P(None, ('tile', 'slab'))
- peak: float32 [2, 32], P(None, ('tile', 'slab'))
The draws below stay inside these ranges and needn't reach their ends.
All inputs are finite; a program needn't handle non-finite values.
Results may differ from the reference program's by a relative error of at most 0.0003.
Values sent between devices are 32-bit elements; how exact they have to be, the bound alone decides.
A program may use at most 192 MiB of HBM per device.

```python
import jax
import jax.numpy as jnp
from jax import lax

Z = 8
A = 128
L = 1024
BAND = 256
GC = 7
ROUNDS = 2
TILES = 32


def plant(drawn, own_key, smallest, high):
    place = [jax.random.randint(jax.random.fold_in(own_key, axis), (), 0, length) for axis, length in enumerate(drawn.shape)]
    widest = drawn.shape.index(max(drawn.shape))
    next_to = place[:widest] + [(place[widest] + 1) % drawn.shape[widest]] + place[widest + 1:]
    return drawn.at[tuple(place)].set(smallest).at[tuple(next_to)].set(high)


def block_levels(rng, dims, shards, smallest, largest):
    gain = 1.0
    for dim, shards_of in shards:
        steps = jax.random.uniform(jax.random.fold_in(jax.random.fold_in(rng, 6), dim), (shards_of,), jnp.float32, smallest / len(shards), largest / len(shards))
        gain = gain * jnp.repeat(jnp.exp(steps), dims[dim] // shards_of).reshape((-1,) + (1,) * (len(dims) - 1 - dim))
    return gain


def noise(own_key, dims, deviation, limit, shards=(), kind=jnp.bfloat16):
    drawn = jax.random.normal(own_key, dims, jnp.float32) * deviation
    if len(shards) > 0:
        drawn = block_levels(own_key, dims, shards, -0.22, 0.18) * drawn
    return jnp.clip(drawn, min=-limit, max=limit).astype(kind)


def setup_inputs(seed: int = 0) -> dict:
    arg_keys = jax.random.split(jax.random.key(seed), 3)
    return {
        "stored": noise(arg_keys[0], (TILES, Z, BAND, L), 1.0, 6.0, ((0, 8), (1, 4)), jnp.float32),
        "offsets": plant(jax.random.randint(arg_keys[1], (ROUNDS, 2, TILES), 0, BAND - A + 1), jax.random.fold_in(arg_keys[1], 1), 0, BAND - A).astype(jnp.int32),
    }


FLOOR = 0.25


def correlate(own_strip, partner_strip):
    spec_own = jnp.fft.fftn(own_strip, norm="ortho")
    spec_partner = jnp.fft.fftn(partner_strip, norm="ortho")
    cross = spec_own * jnp.conj(spec_partner)
    denom = jnp.maximum(jnp.abs(cross), FLOOR)
    field = jnp.real(jnp.fft.ifftn(cross / denom, norm="ortho"))
    return jnp.max(field, axis=0)


def reference(stored, offsets):
    tile_ids = jnp.arange(TILES, dtype=jnp.int32)
    zero = jnp.int32(0)
    surfaces = []
    for rnd in range(ROUNDS):
        stride = 1 if rnd == 0 else GC

        def one_pair(tile):
            partner = jnp.minimum(tile + stride, TILES - 1).astype(jnp.int32)
            if rnd == 0:
                valid = jnp.logical_and((tile % GC) != (GC - 1), (tile + 1) < TILES)
            else:
                valid = (tile + GC) < TILES
            own_strip = lax.dynamic_slice(stored[tile], (zero, offsets[rnd, 0, tile].astype(jnp.int32), zero), (Z, A, L))
            partner_strip = lax.dynamic_slice(stored[partner], (zero, offsets[rnd, 1, partner].astype(jnp.int32), zero), (Z, A, L))
            partner_strip = partner_strip * valid.astype(stored.dtype)
            return correlate(own_strip, partner_strip)

        surfaces.append(lax.map(one_pair, tile_ids))
    surface = jnp.stack(surfaces)
    peak = jnp.max(surface, axis=(2, 3))
    return surface, peak
```

```python
import functools
import math

import jax
import jax.numpy as jnp
import numpy as np
from jax import lax
from jax.experimental import pallas as pl
from jax.experimental.pallas import tpu as pltpu
from jax.sharding import PartitionSpec as P

A = 128
GC = 7
ROUNDS = 2
FLOOR = 0.25
LANES = 128
F32 = jnp.float32
BF16 = jnp.bfloat16


def halves(table):
    high = table.astype(np.float32).astype(BF16)
    low = (table - high.astype(np.float64)).astype(np.float32).astype(BF16)
    return jnp.asarray(high), jnp.asarray(low)


def phases(rows, cols, total):
    angle = (np.outer(rows, cols) % total) * (2.0 * math.pi / total)
    return np.cos(angle), np.sin(angle)


def make_tables(depth, across, along):
    quarter = along // 4
    half = quarter // 2
    scale = 1.0 / math.sqrt(depth * across * along)
    at = np.arange(quarter)
    cos0, sin0 = phases(at, 4 * np.arange(half), along)
    sin0 = -sin0
    sin0[:, 0] = np.where(at % 2 == 0, 1.0, -1.0)
    first = np.concatenate((cos0, sin0), axis=1) * scale
    cos2, sin2 = phases(at, 4 * np.arange(half) + 2, along)
    second = np.concatenate((cos2, -sin2), axis=1) * scale
    cos1, sin1 = phases(at, 4 * np.arange(quarter) + 1, along)
    third = np.block([[cos1, -sin1], [-sin1, -cos1]]) * scale
    weight = np.full((2 * half, 1), 2.0)
    weight[0] = weight[half] = 1.0
    cos_a, sin_a = phases(np.arange(across), np.arange(across), across)
    rows = np.block([[cos_a, sin_a], [-sin_a, cos_a]])
    cos_z, sin_z = phases(np.arange(depth), np.arange(depth), depth)
    planes = np.zeros((2 * LANES, 2 * LANES))
    planes[:depth, :depth] = cos_z
    planes[:depth, LANES : LANES + depth] = -sin_z
    planes[LANES : LANES + depth, :depth] = sin_z
    planes[LANES : LANES + depth, LANES : LANES + depth] = cos_z
    forth = [first, second, third, rows, planes]
    back = [first.T * weight, second.T * 2.0, third.T * 2.0, rows.T, planes.T]
    flat = lambda group: [part for table in group for part in halves(table)]
    return flat(forth), flat(back)


def split(x):
    high = x.astype(BF16)
    return high, (x - high.astype(F32)).astype(BF16)


def dot(a, b):
    return jnp.dot(a, b, preferred_element_type=F32)


def by_right(x, high, low):
    xh, xl = split(x)
    return dot(xh, high[...]) + (dot(xl, high[...]) + dot(xh, low[...]))


def by_left(high, low, x):
    xh, xl = split(x)
    return dot(high[...], xh) + (dot(high[...], xl) + dot(low[...], xh))


def fft(points, sign):
    n = len(points)
    if n == 1:
        return points
    even = fft(points[0::2], sign)
    odd = fft(points[1::2], sign)
    out = [None] * n
    for k in range(n // 2):
        re, im = odd[k]
        if k == 0:
            pass
        elif 4 * k == n:
            re, im = (-im, re) if sign > 0 else (im, -re)
        elif 8 * k == n:
            r = math.sqrt(0.5)
            re, im = ((re - im) * r, (im + re) * r) if sign > 0 else ((re + im) * r, (im - re) * r)
        elif 8 * k == 3 * n:
            r = math.sqrt(0.5)
            re, im = ((-re - im) * r, (re - im) * r) if sign > 0 else ((im - re) * r, (-im - re) * r)
        else:
            c = math.cos(2.0 * math.pi * k / n)
            s = sign * math.sin(2.0 * math.pi * k / n)
            re, im = re * c - im * s, im * c + re * s
        out[k] = (even[k][0] + re, even[k][1] + im)
        out[k + n // 2] = (even[k][0] - re, even[k][1] - im)
    return out


def whiten(own, partner, keep):
    re = own[0] * partner[0] + own[1] * partner[1]
    im = own[1] * partner[0] - own[0] * partner[1]
    gain = lax.rsqrt(jnp.maximum(re * re + im * im, FLOOR * FLOOR)) * keep
    return re * gain, im * gain


def lane_is(shape, lane):
    return lax.broadcasted_iota(jnp.int32, shape, 1) == lane


def spectrum(strip, tabs, spec, edge, column):
    f0h, f0l, f2h, f2l, f1h, f1l, rh, rl, zh, zl = tabs
    depth, across, along = strip.shape
    q = along // 4
    h = q // 2
    column[...] = jnp.zeros_like(column)

    def step(i, carry):
        x = strip[pl.ds(2 * i, 2)].reshape(2 * across, along)
        x0, x1, x2, x3 = (x[:, n * q : (n + 1) * q] for n in range(4))
        s02, s13 = x0 + x2, x1 + x3
        out0 = by_right(s02 + s13, f0h, f0l)
        out2 = by_right(s02 - s13, f2h, f2l)
        out1 = by_right(jnp.concatenate((x0 - x2, x1 - x3), axis=1), f1h, f1l)
        imag0 = out0[:, h:]
        first = lane_is(imag0.shape, 0)
        real = jnp.concatenate((out0[:, :h], out2[:, :h], out1[:, :q]), axis=1)
        imag = jnp.concatenate((jnp.where(first, 0.0, imag0), out2[:, h:], out1[:, q:]), axis=1)
        for n in range(2):
            rows = slice(n * across, (n + 1) * across)
            at = 2 * i + n
            packed = jnp.concatenate((real[rows], imag[rows]), axis=0)
            spec[at] = by_left(rh, rl, packed)
            middle = jnp.broadcast_to(imag0[rows, 0:1], column.shape)
            column[...] = jnp.where(lane_is(column.shape, at), middle, column[...])
        return carry

    lax.fori_loop(0, depth // 2, step, 0)
    turned = by_left(rh.at[:, :across], rl.at[:, :across], column[...])
    turned = jnp.concatenate((turned[:across], turned[across:]), axis=1)
    edge[...] = by_right(turned, zh, zl)


def spectrum_kernel(strip, *refs):
    tabs, (spec, edge, column) = refs[:10], refs[10:]
    spectrum(strip, tabs, spec, edge, column)


def pair_kernel(keep_ref, strip, own, own_edge, *refs):
    forth, back = refs[:10], refs[10:20]
    surface, peak, spec, edge, column = refs[20:]
    b0h, b0l, b2h, b2l, b1h, b1l, rh, rl, zh, zl = back
    depth, across, along = strip.shape
    q = along // 4
    h = q // 2
    spectrum(strip, forth, spec, edge, column)
    keep = keep_ref[0]

    def meet(i, carry):
        re_rows = pl.ds(pl.multiple_of(8 * i, 8), 8)
        im_rows = pl.ds(pl.multiple_of(across + 8 * i, 8), 8)
        for lane in range(0, along // 2, LANES):
            lanes = slice(lane, lane + LANES)
            mine = fft([(own[z, re_rows, lanes], own[z, im_rows, lanes]) for z in range(depth)], -1)
            other = fft([(spec[z, re_rows, lanes], spec[z, im_rows, lanes]) for z in range(depth)], -1)
            white = [whiten(a, b, keep) for a, b in zip(mine, other)]
            for z, (re, im) in enumerate(fft(white, 1)):
                spec[z, re_rows, lanes] = re
                spec[z, im_rows, lanes] = im
        return carry

    lax.fori_loop(0, across // 8, meet, 0)
    re, im = whiten(
        (own_edge[:, :LANES], own_edge[:, LANES:]), (edge[:, :LANES], edge[:, LANES:]), keep
    )
    back_z = by_right(jnp.concatenate((re, im), axis=1), zh, zl)
    back_z = jnp.concatenate((back_z[:, :LANES], back_z[:, LANES:]), axis=0)
    column[...] = by_left(rh.at[:across], rl.at[:across], back_z)

    surface[...] = jnp.full_like(surface, -jnp.inf)

    def step(i, carry):
        parts = []
        for n in range(2):
            at = 2 * i + n
            plane = by_left(rh, rl, spec[at])
            middle = jnp.sum(
                jnp.where(lane_is(column.shape, at), column[...], 0.0), axis=1, keepdims=True
            )
            imag0 = plane[across:, :h]
            imag0 = jnp.where(lane_is(imag0.shape, 0), middle, imag0)
            parts.append((plane[:across], imag0, plane[across:, h:]))
        real = jnp.concatenate([p[0] for p in parts], axis=0)
        imag0 = jnp.concatenate([p[1] for p in parts], axis=0)
        imag = jnp.concatenate([p[2] for p in parts], axis=0)
        z0 = by_right(jnp.concatenate((real[:, :h], imag0), axis=1), b0h, b0l)
        z2 = by_right(jnp.concatenate((real[:, h:q], imag[:, :h]), axis=1), b2h, b2l)
        z1 = by_right(jnp.concatenate((real[:, q:], imag[:, h:]), axis=1), b1h, b1l)
        plus, minus = z0 + z2, z0 - z2
        a, b = z1[:, :q], z1[:, q:]
        for n, part in enumerate((plus + a, minus + b, plus - a, minus - b)):
            lanes = slice(n * q, (n + 1) * q)
            best = jnp.maximum(part[:across], part[across:])
            surface[:, lanes] = jnp.maximum(surface[:, lanes], best)
        return carry

    lax.fori_loop(0, depth // 2, step, 0)
    peak[...] = jnp.broadcast_to(jnp.max(surface[...]), peak.shape)


VMEM = pl.BlockSpec(memory_space=pltpu.VMEM)
SMEM = pl.BlockSpec(memory_space=pltpu.SMEM)
PARAMS = pltpu.CompilerParams(vmem_limit_bytes=56 * 1024 * 1024)


def spectrum_of(strip, forth):
    depth, across, along = strip.shape
    return pl.pallas_call(
        spectrum_kernel,
        out_shape=(
            jax.ShapeDtypeStruct((depth, 2 * across, along // 2), F32),
            jax.ShapeDtypeStruct((across, 2 * LANES), F32),
        ),
        in_specs=[VMEM] * (1 + len(forth)),
        out_specs=(VMEM, VMEM),
        scratch_shapes=[pltpu.VMEM((across, LANES), F32)],
        compiler_params=PARAMS,
        cost_estimate=pl.CostEstimate(flops=8 * 10**9, bytes_accessed=2 * strip.size * 4, transcendentals=0),
    )(strip, *forth)


def pair_of(keep, strip, own, own_edge, forth, back):
    depth, across, along = strip.shape
    return pl.pallas_call(
        pair_kernel,
        out_shape=(
            jax.ShapeDtypeStruct((across, along), F32),
            jax.ShapeDtypeStruct((8, LANES), F32),
        ),
        in_specs=[SMEM] + [VMEM] * (3 + len(forth) + len(back)),
        out_specs=(VMEM, VMEM),
        scratch_shapes=[
            pltpu.VMEM((depth, 2 * across, along // 2), F32),
            pltpu.VMEM((across, 2 * LANES), F32),
            pltpu.VMEM((across, LANES), F32),
        ],
        compiler_params=PARAMS,
        cost_estimate=pl.CostEstimate(flops=16 * 10**9, bytes_accessed=2 * strip.size * 4, transcendentals=0),
    )(keep, strip, own, own_edge, *forth, *back)


def from_behind(x, axis, by):
    size = lax.axis_size(axis)
    pairs = [(i, i + by) for i in range(size) if 0 <= i + by < size]
    return lax.ppermute(x, axis, pairs)


def on_device(stored, offsets):
    axes = ("tile", "slab")
    owned = lax.all_to_all(stored, "slab", split_axis=0, concat_axis=1, tiled=True)[0]
    depth, _, along = owned.shape
    forth, back = make_tables(depth, A, along)
    count = lax.axis_size(axes)
    place = lax.axis_index(axes)
    cut = lambda rnd, which: lax.dynamic_slice_in_dim(owned, offsets[rnd, which, 0], A, 1)
    arrived = [from_behind(cut(rnd, 1), axes, -(1 if rnd == 0 else GC)) for rnd in range(ROUNDS)]
    own = [spectrum_of(cut(rnd, 0), forth) for rnd in range(ROUNDS)]
    surfaces, peaks = [], []
    for rnd in range(ROUNDS):
        if rnd == 0:
            valid = jnp.logical_and(place % GC != GC - 1, place + 1 < count)
        else:
            valid = place + GC < count
        surface, peak = pair_of(
            valid.astype(F32).reshape(1), arrived[rnd], *own[rnd], forth, back
        )
        surfaces.append(surface)
        peaks.append(peak[0, 0])
    return jnp.stack(surfaces)[:, None], jnp.stack(peaks)[:, None]


def solution(mesh):
    return jax.shard_map(
        on_device,
        mesh=mesh,
        in_specs=(P("tile", "slab", None, None), P(None, None, ("tile", "slab"))),
        out_specs=(P(None, ("tile", "slab"), None, None), P(None, ("tile", "slab"))),
        check_vma=False,
    )
```

```python
import functools
import math

import jax
import jax.numpy as jnp
import numpy as np
from jax import lax
from jax.experimental import pallas as pl
from jax.experimental.pallas import tpu as pltpu
from jax.sharding import PartitionSpec as P

A = 128
GC = 7
ROUNDS = 2
PER_CHIP = 2
FLOOR = 0.25
LANES = 128
F32 = jnp.float32
BF16 = jnp.bfloat16


def halves(table):
    high = table.astype(np.float32).astype(BF16)
    low = (table - high.astype(np.float64)).astype(np.float32).astype(BF16)
    return jnp.asarray(high), jnp.asarray(low)


def phases(rows, cols, total):
    angle = (np.outer(rows, cols) % total) * (2.0 * math.pi / total)
    return np.cos(angle), np.sin(angle)


def make_tables(depth, across, along):
    quarter = along // 4
    half = quarter // 2
    scale = 1.0 / math.sqrt(depth * across * along)
    at = np.arange(quarter)
    cos0, sin0 = phases(at, 4 * np.arange(half), along)
    sin0 = -sin0
    sin0[:, 0] = np.where(at % 2 == 0, 1.0, -1.0)
    first = np.concatenate((cos0, sin0), axis=1) * scale
    cos2, sin2 = phases(at, 4 * np.arange(half) + 2, along)
    second = np.concatenate((cos2, -sin2), axis=1) * scale
    cos1, sin1 = phases(at, 4 * np.arange(quarter) + 1, along)
    third = np.block([[cos1, -sin1], [-sin1, -cos1]]) * scale
    weight = np.full((2 * half, 1), 2.0)
    weight[0] = weight[half] = 1.0
    cos_a, sin_a = phases(np.arange(across), np.arange(across), across)
    rows = np.block([[cos_a, sin_a], [-sin_a, cos_a]])
    cos_z, sin_z = phases(np.arange(depth), np.arange(depth), depth)
    planes = np.zeros((2 * LANES, 2 * LANES))
    planes[:depth, :depth] = cos_z
    planes[:depth, LANES : LANES + depth] = -sin_z
    planes[LANES : LANES + depth, :depth] = sin_z
    planes[LANES : LANES + depth, LANES : LANES + depth] = cos_z
    forth = [first, second, third, rows, planes]
    back = [first.T * weight, second.T * 2.0, third.T * 2.0, rows.T, planes.T]
    flat = lambda group: [part for table in group for part in halves(table)]
    return flat(forth), flat(back)


def split(x):
    high = x.astype(BF16)
    return high, (x - high.astype(F32)).astype(BF16)


def dot(a, b):
    return jnp.dot(a, b, preferred_element_type=F32)


def by_right(x, high, low):
    xh, xl = split(x)
    return dot(xh, high[...]) + (dot(xl, high[...]) + dot(xh, low[...]))


def by_left(high, low, x):
    xh, xl = split(x)
    return dot(high[...], xh) + (dot(high[...], xl) + dot(low[...], xh))


def fft(points, sign):
    n = len(points)
    if n == 1:
        return points
    even = fft(points[0::2], sign)
    odd = fft(points[1::2], sign)
    out = [None] * n
    for k in range(n // 2):
        re, im = odd[k]
        if k == 0:
            pass
        elif 4 * k == n:
            re, im = (-im, re) if sign > 0 else (im, -re)
        elif 8 * k == n:
            r = math.sqrt(0.5)
            re, im = ((re - im) * r, (im + re) * r) if sign > 0 else ((re + im) * r, (im - re) * r)
        elif 8 * k == 3 * n:
            r = math.sqrt(0.5)
            re, im = ((-re - im) * r, (re - im) * r) if sign > 0 else ((im - re) * r, (-im - re) * r)
        else:
            c = math.cos(2.0 * math.pi * k / n)
            s = sign * math.sin(2.0 * math.pi * k / n)
            re, im = re * c - im * s, im * c + re * s
        out[k] = (even[k][0] + re, even[k][1] + im)
        out[k + n // 2] = (even[k][0] - re, even[k][1] - im)
    return out


def whiten(own, partner):
    re = own[0] * partner[0] + own[1] * partner[1]
    im = own[1] * partner[0] - own[0] * partner[1]
    gain = lax.rsqrt(jnp.maximum(re * re + im * im, FLOOR * FLOOR))
    return re * gain, im * gain


def lane_is(shape, lane):
    return lax.broadcasted_iota(jnp.int32, shape, 1) == lane


def spectrum_kernel(slot, count, *refs):
    strips, (f0h, f0l, f2h, f2l, f1h, f1l, rh, rl) = refs[:count], refs[count : count + 8]
    spec, column = refs[count + 8 :]
    depth, across, along = strips[0].shape
    q = along // 4
    h = q // 2
    x = sum(strip[...] for strip in strips).reshape(depth * across, along)
    x0, x1, x2, x3 = (x[:, n * q : (n + 1) * q] for n in range(4))
    s02, s13 = x0 + x2, x1 + x3
    out0 = by_right(s02 + s13, f0h, f0l)
    out2 = by_right(s02 - s13, f2h, f2l)
    out1 = by_right(jnp.concatenate((x0 - x2, x1 - x3), axis=1), f1h, f1l)
    imag0 = out0[:, h:]
    first = lane_is(imag0.shape, 0)
    real = jnp.concatenate((out0[:, :h], out2[:, :h], out1[:, :q]), axis=1)
    imag = jnp.concatenate((jnp.where(first, 0.0, imag0), out2[:, h:], out1[:, q:]), axis=1)
    middles = jnp.zeros(column.shape, F32)
    for n in range(depth):
        rows = slice(n * across, (n + 1) * across)
        spec[n] = by_left(rh, rl, jnp.concatenate((real[rows], imag[rows]), axis=0))
        middle = jnp.broadcast_to(imag0[rows, 0:1], column.shape)
        middles = jnp.where(lane_is(column.shape, slot * depth + n), middle, middles)
    column[...] = middles


def pair_kernel(parts, *refs):
    own, other = refs[:parts], refs[parts : 2 * parts]
    own_cols, other_cols = refs[2 * parts : 3 * parts], refs[3 * parts : 4 * parts]
    (ah, al, zh, zl), back = refs[4 * parts : 4 * parts + 4], refs[4 * parts + 4 : 4 * parts + 14]
    surface, spec, column = refs[4 * parts + 14 :]
    b0h, b0l, b2h, b2l, b1h, b1l, rh, rl, bzh, bzl = back
    per = own[0].shape[0]
    depth = per * parts
    across, along = surface.shape
    q = along // 4
    h = q // 2

    def meet(i, carry):
        re_rows = pl.ds(pl.multiple_of(8 * i, 8), 8)
        im_rows = pl.ds(pl.multiple_of(across + 8 * i, 8), 8)
        for lane in range(0, along // 2, LANES):
            lanes = slice(lane, lane + LANES)
            load = lambda group: [
                (group[z // per][z % per, re_rows, lanes], group[z // per][z % per, im_rows, lanes])
                for z in range(depth)
            ]
            white = [whiten(a, b) for a, b in zip(fft(load(own), -1), fft(load(other), -1))]
            for z, (re, im) in enumerate(fft(white, 1)):
                spec[z, re_rows, lanes] = re
                spec[z, im_rows, lanes] = im
        return carry

    lax.fori_loop(0, across // 8, meet, 0)

    def edge(group):
        turned = by_left(ah.at[:, :across], al.at[:, :across], sum(c[...] for c in group))
        turned = by_right(jnp.concatenate((turned[:across], turned[across:]), axis=1), zh, zl)
        return turned[:, :LANES], turned[:, LANES:]

    white = whiten(edge(own_cols), edge(other_cols))
    back_z = by_right(jnp.concatenate(white, axis=1), bzh, bzl)
    back_z = jnp.concatenate((back_z[:, :LANES], back_z[:, LANES:]), axis=0)
    column[...] = by_left(rh.at[:across], rl.at[:across], back_z)

    surface[...] = jnp.full(surface.shape, -jnp.inf, F32)

    def step(i, carry):
        planes = []
        for n in range(2):
            at = 2 * i + n
            plane = by_left(rh, rl, spec[at])
            middle = jnp.sum(
                jnp.where(lane_is(column.shape, at), column[...], 0.0), axis=1, keepdims=True
            )
            imag0 = plane[across:, :h]
            imag0 = jnp.where(lane_is(imag0.shape, 0), middle, imag0)
            planes.append((plane[:across], imag0, plane[across:, h:]))
        real, imag0, imag = (jnp.concatenate(group, axis=0) for group in zip(*planes))
        z0 = by_right(jnp.concatenate((real[:, :h], imag0), axis=1), b0h, b0l)
        z2 = by_right(jnp.concatenate((real[:, h:q], imag[:, :h]), axis=1), b2h, b2l)
        z1 = by_right(jnp.concatenate((real[:, q:], imag[:, h:]), axis=1), b1h, b1l)
        plus, minus = z0 + z2, z0 - z2
        a, b = z1[:, :q], z1[:, q:]
        for n, part in enumerate((plus + a, minus + b, plus - a, minus - b)):
            lanes = slice(n * q, (n + 1) * q)
            best = jnp.maximum(part[:across], part[across:])
            surface[:, lanes] = jnp.maximum(surface[:, lanes], best)
        return carry

    lax.fori_loop(0, depth // 2, step, 0)


VMEM = pl.BlockSpec(memory_space=pltpu.VMEM)
PARAMS = pltpu.CompilerParams(vmem_limit_bytes=48 * 1024 * 1024)


def spectrum_of(strips, slot, forth):
    depth, across, along = strips[0].shape
    return pl.pallas_call(
        functools.partial(spectrum_kernel, slot, len(strips)),
        out_shape=(
            jax.ShapeDtypeStruct((depth, 2 * across, along // 2), F32),
            jax.ShapeDtypeStruct((across, LANES), F32),
        ),
        in_specs=[VMEM] * (len(strips) + 8),
        out_specs=(VMEM, VMEM),
        compiler_params=PARAMS,
        cost_estimate=pl.CostEstimate(
            flops=2 * 10**9, bytes_accessed=16 * 10**6, transcendentals=0
        ),
    )(*strips, *forth[:8])


def pair_of(own, other, forth, back):
    parts = len(own)
    per, rows, half = own[0][0].shape
    across, along = rows // 2, 2 * half
    operands = [x[0] for x in own] + [x[0] for x in other] + [x[1] for x in own] + [x[1] for x in other]
    operands += forth[6:10] + back
    return pl.pallas_call(
        functools.partial(pair_kernel, parts),
        out_shape=jax.ShapeDtypeStruct((across, along), F32),
        in_specs=[VMEM] * len(operands),
        out_specs=VMEM,
        scratch_shapes=[
            pltpu.VMEM((parts * per, rows, half), F32),
            pltpu.VMEM((across, LANES), F32),
        ],
        compiler_params=PARAMS,
        cost_estimate=pl.CostEstimate(
            flops=12 * 10**9, bytes_accessed=36 * 10**6, transcendentals=0
        ),
    )(*operands)


def on_device(stored, offsets):
    axes = ("tile", "slab")
    slabs = lax.axis_size("slab")
    count = lax.axis_size(axes)
    group = PER_CHIP * slabs
    per, along = stored.shape[1], stored.shape[3]
    forth, back = make_tables(per * slabs, A, along)
    strides = (1, GC)

    def place_of(t):
        inside = t % group
        return (t // group * PER_CHIP + inside % PER_CHIP) * slabs + inside // PER_CHIP

    def giver(rnd, t):
        to = t - strides[rnd]
        return to >= 0 and (rnd == 1 or to % GC != GC - 1)

    def same_slab(rnd, t):
        return place_of(t) % slabs == place_of(t - strides[rnd]) % slabs

    slab = lax.axis_index("slab")
    everyone = lax.all_gather(offsets[:, 1, 0], "slab")
    mine = lax.ppermute(offsets[:, :, 0], axes, [(t, place_of(t)) for t in range(count)])

    def cut(planes, at):
        return lax.dynamic_slice_in_dim(planes, at, A, 1)

    own = [[None] * slabs for _ in range(ROUNDS)]
    other = [[None] * slabs for _ in range(ROUNDS)]
    bands = []
    direct = [[None] * slabs for _ in range(ROUNDS)]
    for step in range(slabs):
        holder = lambda t: t // slabs * slabs + (t - step) % slabs
        which = (slab + step) % slabs
        planes = lax.dynamic_index_in_dim(stored, which, 0, False)
        bands.append(lax.ppermute(planes, axes, [(holder(t), place_of(t)) for t in range(count)]))
        for rnd in range(ROUNDS):
            pairs = [
                (holder(t), place_of(t - strides[rnd]))
                for t in range(count)
                if giver(rnd, t) and not same_slab(rnd, t)
            ]
            at = lax.dynamic_index_in_dim(everyone, which, 0, False)[rnd]
            direct[rnd][step] = lax.ppermute(cut(planes, at), axes, pairs)
    for step in range(slabs):
        slot = slabs - 1 - step
        for rnd in range(ROUNDS):
            own[rnd][slot] = spectrum_of([cut(bands[step], mine[rnd, 0])], slot, forth)
            pairs = [
                (place_of(t), place_of(t - strides[rnd]))
                for t in range(count)
                if giver(rnd, t) and same_slab(rnd, t)
            ]
            near = lax.ppermute(cut(bands[step], mine[rnd, 1]), axes, pairs)
            slot_there = slabs - 1 - (step - strides[rnd]) % slabs
            other[rnd][slot_there] = spectrum_of([near, direct[rnd][step]], slot_there, forth)
    surfaces = []
    for rnd in range(ROUNDS):
        surface = pair_of(own[rnd], other[rnd], forth, back)
        home = lax.ppermute(surface, axes, [(place_of(t), t) for t in range(count)])
        surfaces.append(home)
    surface = jnp.stack(surfaces)[:, None]
    return surface, jnp.max(surface, axis=(2, 3))


def solution(mesh):
    return jax.shard_map(
        on_device,
        mesh=mesh,
        in_specs=(P("tile", "slab", None, None), P(None, None, ("tile", "slab"))),
        out_specs=(P(None, ("tile", "slab"), None, None), P(None, ("tile", "slab"))),
        check_vma=False,
    )
```

```python
import functools
import math

import jax
import jax.numpy as jnp
import numpy as np
from jax import lax
from jax.experimental import pallas as pl
from jax.experimental.pallas import tpu as pltpu
from jax.sharding import PartitionSpec as P

A = 128
GC = 7
ROUNDS = 2
PER_CHIP = 2
FLOOR = 0.25
LANES = 128
F32 = jnp.float32
BF16 = jnp.bfloat16


def halves(table):
    high = table.astype(np.float32).astype(BF16)
    low = (table - high.astype(np.float64)).astype(np.float32).astype(BF16)
    return jnp.asarray(high), jnp.asarray(low)


def phases(rows, cols, total):
    angle = (np.outer(rows, cols) % total) * (2.0 * math.pi / total)
    return np.cos(angle), np.sin(angle)


def make_tables(depth, across, along):
    quarter = along // 4
    half = quarter // 2
    scale = 1.0 / math.sqrt(depth * across * along)
    at = np.arange(quarter)
    cos0, sin0 = phases(at, 4 * np.arange(half), along)
    sin0 = -sin0
    sin0[:, 0] = np.where(at % 2 == 0, 1.0, -1.0)
    first = np.concatenate((cos0, sin0), axis=1) * scale
    cos2, sin2 = phases(at, 4 * np.arange(half) + 2, along)
    second = np.concatenate((cos2, -sin2), axis=1) * scale
    cos1, sin1 = phases(at, 4 * np.arange(quarter) + 1, along)
    third = np.block([[cos1, -sin1], [-sin1, -cos1]]) * scale
    weight = np.full((2 * half, 1), 2.0)
    weight[0] = weight[half] = 1.0
    cos_a, sin_a = phases(np.arange(across), np.arange(across), across)
    rows = np.block([[cos_a, sin_a], [-sin_a, cos_a]])
    cos_z, sin_z = phases(np.arange(depth), np.arange(depth), depth)
    planes = np.zeros((2 * LANES, 2 * LANES))
    planes[:depth, :depth] = cos_z
    planes[:depth, LANES : LANES + depth] = -sin_z
    planes[LANES : LANES + depth, :depth] = sin_z
    planes[LANES : LANES + depth, LANES : LANES + depth] = cos_z
    forth = [first, second, third, rows, planes]
    back = [first.T * weight, second.T * 2.0, third.T * 2.0, rows.T, planes.T]
    flat = lambda group: [part for table in group for part in halves(table)]
    return flat(forth), flat(back)


def split(x):
    high = x.astype(BF16)
    return high, (x - high.astype(F32)).astype(BF16)


def dot(a, b):
    return jnp.dot(a, b, preferred_element_type=F32)


def by_right(x, high, low):
    xh, xl = split(x)
    return dot(xh, high[...]) + (dot(xl, high[...]) + dot(xh, low[...]))


def by_left(high, low, x):
    xh, xl = split(x)
    return dot(high[...], xh) + (dot(high[...], xl) + dot(low[...], xh))


def fft(points, sign):
    n = len(points)
    if n == 1:
        return points
    even = fft(points[0::2], sign)
    odd = fft(points[1::2], sign)
    out = [None] * n
    for k in range(n // 2):
        re, im = odd[k]
        if k == 0:
            pass
        elif 4 * k == n:
            re, im = (-im, re) if sign > 0 else (im, -re)
        elif 8 * k == n:
            r = math.sqrt(0.5)
            re, im = ((re - im) * r, (im + re) * r) if sign > 0 else ((re + im) * r, (im - re) * r)
        elif 8 * k == 3 * n:
            r = math.sqrt(0.5)
            re, im = ((-re - im) * r, (re - im) * r) if sign > 0 else ((im - re) * r, (-im - re) * r)
        else:
            c = math.cos(2.0 * math.pi * k / n)
            s = sign * math.sin(2.0 * math.pi * k / n)
            re, im = re * c - im * s, im * c + re * s
        out[k] = (even[k][0] + re, even[k][1] + im)
        out[k + n // 2] = (even[k][0] - re, even[k][1] - im)
    return out


def whiten(own, partner):
    re = own[0] * partner[0] + own[1] * partner[1]
    im = own[1] * partner[0] - own[0] * partner[1]
    gain = lax.rsqrt(jnp.maximum(re * re + im * im, FLOOR * FLOOR))
    return re * gain, im * gain


def lane_is(shape, lane):
    return lax.broadcasted_iota(jnp.int32, shape, 1) == lane


def spectrum_kernel(slot, count, *refs):
    strips, (f0h, f0l, f2h, f2l, f1h, f1l, rh, rl) = refs[:count], refs[count : count + 8]
    spec, column = refs[count + 8 :]
    depth, across, along = strips[0].shape
    q = along // 4
    h = q // 2
    x = sum(strip[...] for strip in strips).reshape(depth * across, along)
    x0, x1, x2, x3 = (x[:, n * q : (n + 1) * q] for n in range(4))
    s02, s13 = x0 + x2, x1 + x3
    out0 = by_right(s02 + s13, f0h, f0l)
    out2 = by_right(s02 - s13, f2h, f2l)
    out1 = by_right(jnp.concatenate((x0 - x2, x1 - x3), axis=1), f1h, f1l)
    imag0 = out0[:, h:]
    first = lane_is(imag0.shape, 0)
    real = jnp.concatenate((out0[:, :h], out2[:, :h], out1[:, :q]), axis=1)
    imag = jnp.concatenate((jnp.where(first, 0.0, imag0), out2[:, h:], out1[:, q:]), axis=1)
    middles = jnp.zeros(column.shape, F32)
    for n in range(depth):
        rows = slice(n * across, (n + 1) * across)
        spec[n] = by_left(rh, rl, jnp.concatenate((real[rows], imag[rows]), axis=0))
        middle = jnp.broadcast_to(imag0[rows, 0:1], column.shape)
        middles = jnp.where(lane_is(column.shape, slot * depth + n), middle, middles)
    column[...] = middles


def pair_kernel(parts, *refs):
    own, other = refs[:parts], refs[parts : 2 * parts]
    own_cols, other_cols = refs[2 * parts : 3 * parts], refs[3 * parts : 4 * parts]
    (ah, al, zh, zl), back = refs[4 * parts : 4 * parts + 4], refs[4 * parts + 4 : 4 * parts + 14]
    surface, spec, column = refs[4 * parts + 14 :]
    b0h, b0l, b2h, b2l, b1h, b1l, rh, rl, bzh, bzl = back
    per = own[0].shape[0]
    depth = per * parts
    across, along = surface.shape
    q = along // 4
    h = q // 2

    def meet(i, carry):
        re_rows = pl.ds(pl.multiple_of(8 * i, 8), 8)
        im_rows = pl.ds(pl.multiple_of(across + 8 * i, 8), 8)
        for lane in range(0, along // 2, LANES):
            lanes = slice(lane, lane + LANES)
            load = lambda group: [
                (group[z // per][z % per, re_rows, lanes], group[z // per][z % per, im_rows, lanes])
                for z in range(depth)
            ]
            white = [whiten(a, b) for a, b in zip(fft(load(own), -1), fft(load(other), -1))]
            for z, (re, im) in enumerate(fft(white, 1)):
                spec[z, re_rows, lanes] = re
                spec[z, im_rows, lanes] = im
        return carry

    lax.fori_loop(0, across // 8, meet, 0)

    def edge(group):
        turned = by_left(ah.at[:, :across], al.at[:, :across], sum(c[...] for c in group))
        turned = by_right(jnp.concatenate((turned[:across], turned[across:]), axis=1), zh, zl)
        return turned[:, :LANES], turned[:, LANES:]

    white = whiten(edge(own_cols), edge(other_cols))
    back_z = by_right(jnp.concatenate(white, axis=1), bzh, bzl)
    back_z = jnp.concatenate((back_z[:, :LANES], back_z[:, LANES:]), axis=0)
    column[...] = by_left(rh.at[:across], rl.at[:across], back_z)

    surface[...] = jnp.full(surface.shape, -jnp.inf, F32)

    def step(i, carry):
        planes = []
        for n in range(2):
            at = 2 * i + n
            plane = by_left(rh, rl, spec[at])
            middle = jnp.sum(
                jnp.where(lane_is(column.shape, at), column[...], 0.0), axis=1, keepdims=True
            )
            imag0 = plane[across:, :h]
            imag0 = jnp.where(lane_is(imag0.shape, 0), middle, imag0)
            planes.append((plane[:across], imag0, plane[across:, h:]))
        real, imag0, imag = (jnp.concatenate(group, axis=0) for group in zip(*planes))
        z0 = by_right(jnp.concatenate((real[:, :h], imag0), axis=1), b0h, b0l)
        z2 = by_right(jnp.concatenate((real[:, h:q], imag[:, :h]), axis=1), b2h, b2l)
        z1 = by_right(jnp.concatenate((real[:, q:], imag[:, h:]), axis=1), b1h, b1l)
        plus, minus = z0 + z2, z0 - z2
        a, b = z1[:, :q], z1[:, q:]
        for n, part in enumerate((plus + a, minus + b, plus - a, minus - b)):
            lanes = slice(n * q, (n + 1) * q)
            best = jnp.maximum(part[:across], part[across:])
            surface[:, lanes] = jnp.maximum(surface[:, lanes], best)
        return carry

    lax.fori_loop(0, depth // 2, step, 0)


VMEM = pl.BlockSpec(memory_space=pltpu.VMEM)
PARAMS = pltpu.CompilerParams(vmem_limit_bytes=48 * 1024 * 1024)


def spectrum_of(strips, slot, forth):
    depth, across, along = strips[0].shape
    return pl.pallas_call(
        functools.partial(spectrum_kernel, slot, len(strips)),
        out_shape=(
            jax.ShapeDtypeStruct((depth, 2 * across, along // 2), F32),
            jax.ShapeDtypeStruct((across, LANES), F32),
        ),
        in_specs=[VMEM] * (len(strips) + 8),
        out_specs=(VMEM, VMEM),
        compiler_params=PARAMS,
        cost_estimate=pl.CostEstimate(
            flops=2 * 10**9, bytes_accessed=16 * 10**6, transcendentals=0
        ),
    )(*strips, *forth[:8])


def pair_of(own, other, forth, back):
    parts = len(own)
    per, rows, half = own[0][0].shape
    across, along = rows // 2, 2 * half
    operands = [x[0] for x in own] + [x[0] for x in other] + [x[1] for x in own] + [x[1] for x in other]
    operands += forth[6:10] + back
    return pl.pallas_call(
        functools.partial(pair_kernel, parts),
        out_shape=jax.ShapeDtypeStruct((across, along), F32),
        in_specs=[VMEM] * len(operands),
        out_specs=VMEM,
        scratch_shapes=[
            pltpu.VMEM((parts * per, rows, half), F32),
            pltpu.VMEM((across, LANES), F32),
        ],
        compiler_params=PARAMS,
        cost_estimate=pl.CostEstimate(
            flops=12 * 10**9, bytes_accessed=36 * 10**6, transcendentals=0
        ),
    )(*operands)


def on_device(stored, offsets):
    axes = ("tile", "slab")
    slabs = lax.axis_size("slab")
    count = lax.axis_size(axes)
    group = PER_CHIP * slabs
    per, along = stored.shape[1], stored.shape[3]
    forth, back = make_tables(per * slabs, A, along)
    strides = (1, GC)

    def place_of(t):
        inside = t % group
        return (t // group * PER_CHIP + inside % PER_CHIP) * slabs + inside // PER_CHIP

    def gives(rnd, t):
        to = t - strides[rnd]
        return to >= 0 and (rnd == 1 or to % GC != GC - 1)

    def holder(t, step, of):
        return t // slabs * slabs + (of - step) % slabs

    near = [(t, t - strides[1 - t % 2]) for t in range(count) if gives(1 - t % 2, t)]
    far = [(t, t - strides[t % 2]) for t in range(count) if gives(t % 2, t)]

    tile, slab = lax.axis_index("tile"), lax.axis_index("slab")
    here = tile // PER_CHIP * group + slab * PER_CHIP + tile % PER_CHIP
    odd = here % 2
    table = lax.all_gather(offsets[:, :, 0], axes)
    stored, table = lax.optimization_barrier((stored, table))

    def cut(planes, at):
        return lax.dynamic_slice_in_dim(planes, at, A, 1)

    bands, fars = [], []
    for step in range(slabs):
        planes = lax.dynamic_index_in_dim(stored, (slab + step) % slabs, 0, False)
        bands.append(
            lax.ppermute(planes, axes, [(holder(t, step, t), place_of(t)) for t in range(count)])
        )
        ahead = (slab + step) % slabs
        which = jnp.where(
            (ahead + strides[0]) % 2 == 0, (ahead + strides[0]) % slabs, (ahead + strides[1]) % slabs
        )
        planes = lax.dynamic_index_in_dim(stored, which, 0, False)
        at = table[tile * slabs + which, which % 2, 1]
        fars.append(
            lax.ppermute(
                cut(planes, at), axes, [(holder(t, step, to), place_of(to)) for t, to in far]
            )
        )

    def spectra(pieces):
        return [spectrum_of([piece], n, forth) for n, piece in enumerate(pieces[::-1])]

    def own(rnd):
        at = table[here, rnd, 0]
        return spectra([cut(band, at) for band in bands])

    def surface_of(rnd, arrived):
        surface = pair_of(own(rnd), spectra(arrived), forth, back)
        return lax.ppermute(surface, axes, [(place_of(t), t) for t in range(count)])

    given = [cut(band, table[here, 1 - odd, 1]) for band in bands]
    nears = [None] * slabs
    for first in (1, 0):
        steps = range(first, slabs, 2)
        ready = [
            jnp.where(odd == 1, given[(s + strides[0]) % slabs], given[(s + strides[1]) % slabs])
            for s in steps
        ]
        pairs = [(place_of(t), place_of(to)) for t, to in near]
        arrived = lax.ppermute(jnp.concatenate(ready), axes, pairs)
        for n, s in enumerate(steps):
            nears[s] = arrived[n * per : (n + 1) * per]
    from_far = surface_of(1 - odd, fars)
    from_near = surface_of(odd, nears)
    home_odd = (tile * slabs + slab) % 2 == 1
    surface = jnp.stack(
        (jnp.where(home_odd, from_far, from_near), jnp.where(home_odd, from_near, from_far))
    )[:, None]
    return surface, jnp.max(surface, axis=(2, 3))


def solution(mesh):
    return jax.shard_map(
        on_device,
        mesh=mesh,
        in_specs=(P("tile", "slab", None, None), P(None, None, ("tile", "slab"))),
        out_specs=(P(None, ("tile", "slab"), None, None), P(None, ("tile", "slab"))),
        check_vma=False,
    )
```

```python
import math

import jax
import jax.numpy as jnp
import numpy as np
from jax import lax
from jax.experimental import pallas as pl
from jax.experimental.pallas import tpu as pltpu
from jax.sharding import PartitionSpec as P

A = 128
GC = 7
ROUNDS = 2
PER_CHIP = 2
FLOOR = 0.25
LANES = 128
F32 = jnp.float32
BF16 = jnp.bfloat16


def halves(table):
    high = table.astype(np.float32).astype(BF16)
    low = (table - high.astype(np.float64)).astype(np.float32).astype(BF16)
    return jnp.asarray(high), jnp.asarray(low)


def phases(rows, cols, total):
    angle = (np.outer(rows, cols) % total) * (2.0 * math.pi / total)
    return np.cos(angle), np.sin(angle)


def make_tables(depth, across, along):
    quarter = along // 4
    half = quarter // 2
    scale = 1.0 / math.sqrt(depth * across * along)
    at = np.arange(quarter)
    cos0, sin0 = phases(at, 4 * np.arange(half), along)
    sin0 = -sin0
    sin0[:, 0] = np.where(at % 2 == 0, 1.0, -1.0)
    first = np.concatenate((cos0, sin0), axis=1) * scale
    cos2, sin2 = phases(at, 4 * np.arange(half) + 2, along)
    second = np.concatenate((cos2, -sin2), axis=1) * scale
    cos1, sin1 = phases(at, 4 * np.arange(quarter) + 1, along)
    third = np.block([[cos1, -sin1], [-sin1, -cos1]]) * scale
    weight = np.full((2 * half, 1), 2.0)
    weight[0] = weight[half] = 1.0
    cos_a, sin_a = phases(np.arange(across), np.arange(across), across)
    rows = np.block([[cos_a, sin_a], [-sin_a, cos_a]])
    cos_z, sin_z = phases(np.arange(depth), np.arange(depth), depth)
    planes = np.zeros((2 * LANES, 2 * LANES))
    planes[:depth, :depth] = cos_z
    planes[:depth, LANES : LANES + depth] = -sin_z
    planes[LANES : LANES + depth, :depth] = sin_z
    planes[LANES : LANES + depth, LANES : LANES + depth] = cos_z
    forth = [first, second, third, rows, planes]
    back = [first.T * weight, second.T * 2.0, third.T * 2.0, rows.T, planes.T]
    flat = lambda group: [part for table in group for part in halves(table)]
    return flat(forth), flat(back)


def split(x):
    high = x.astype(BF16)
    return high, (x - high.astype(F32)).astype(BF16)


def dot(a, b):
    return jnp.dot(a, b, preferred_element_type=F32)


def by_right(x, high, low):
    xh, xl = split(x)
    return dot(xh, high[...]) + (dot(xl, high[...]) + dot(xh, low[...]))


def by_left(high, low, x):
    xh, xl = split(x)
    return dot(high[...], xh) + (dot(high[...], xl) + dot(low[...], xh))


def fft(points, sign):
    n = len(points)
    if n == 1:
        return points
    even = fft(points[0::2], sign)
    odd = fft(points[1::2], sign)
    out = [None] * n
    for k in range(n // 2):
        re, im = odd[k]
        if k == 0:
            pass
        elif 4 * k == n:
            re, im = (-im, re) if sign > 0 else (im, -re)
        elif 8 * k == n:
            r = math.sqrt(0.5)
            re, im = ((re - im) * r, (im + re) * r) if sign > 0 else ((re + im) * r, (im - re) * r)
        elif 8 * k == 3 * n:
            r = math.sqrt(0.5)
            re, im = ((-re - im) * r, (re - im) * r) if sign > 0 else ((im - re) * r, (-im - re) * r)
        else:
            c = math.cos(2.0 * math.pi * k / n)
            s = sign * math.sin(2.0 * math.pi * k / n)
            re, im = re * c - im * s, im * c + re * s
        out[k] = (even[k][0] + re, even[k][1] + im)
        out[k + n // 2] = (even[k][0] - re, even[k][1] - im)
    return out


def whiten(own, partner):
    re = own[0] * partner[0] + own[1] * partner[1]
    im = own[1] * partner[0] - own[0] * partner[1]
    gain = lax.rsqrt(jnp.maximum(re * re + im * im, FLOOR * FLOOR))
    return re * gain, im * gain


def times(a, b):
    return a[0] * b[0] - a[1] * b[1], a[1] * b[0] + a[0] * b[1]


def lane_is(shape, lane):
    return lax.broadcasted_iota(jnp.int32, shape, 1) == lane


def spectrum_kernel(strip, f0h, f0l, f2h, f2l, f1h, f1l, rh, rl, spec, column):
    depth, across, along = strip.shape
    q = along // 4
    h = q // 2
    part = pl.program_id(0)
    x = strip[...].reshape(depth * across, along)
    x0, x1, x2, x3 = (x[:, n * q : (n + 1) * q] for n in range(4))
    s02, s13 = x0 + x2, x1 + x3
    out0 = by_right(s02 + s13, f0h, f0l)
    out2 = by_right(s02 - s13, f2h, f2l)
    out1 = by_right(jnp.concatenate((x0 - x2, x1 - x3), axis=1), f1h, f1l)
    imag0 = out0[:, h:]
    first = lane_is(imag0.shape, 0)
    real = jnp.concatenate((out0[:, :h], out2[:, :h], out1[:, :q]), axis=1)
    imag = jnp.concatenate((jnp.where(first, 0.0, imag0), out2[:, h:], out1[:, q:]), axis=1)
    middles = jnp.where(part == 0, 0.0, column[...])
    for n in range(depth):
        rows = slice(n * across, (n + 1) * across)
        spec[n] = by_left(rh, rl, jnp.concatenate((real[rows], imag[rows]), axis=0))
        middle = jnp.broadcast_to(imag0[rows, 0:1], column.shape)
        middles = jnp.where(lane_is(column.shape, part * depth + n), middle, middles)
    column[...] = middles


def pair_kernel(turn, own, other, own_col, other_col, turn_row, *refs):
    (ah, al, zh, zl), back = refs[:4], refs[4:14]
    surface, spec, column = refs[14:]
    b0h, b0l, b2h, b2l, b1h, b1l, rh, rl, bzh, bzl = back
    depth = own.shape[0]
    across, along = surface.shape
    q = along // 4
    h = q // 2

    def meet(i, carry):
        re_rows = pl.ds(pl.multiple_of(8 * i, 8), 8)
        im_rows = pl.ds(pl.multiple_of(across + 8 * i, 8), 8)
        for lane in range(0, along // 2, LANES):
            lanes = slice(lane, lane + LANES)
            load = lambda held: [(held[z, re_rows, lanes], held[z, im_rows, lanes]) for z in range(depth)]
            theirs = [
                times(point, (turn[0, u], turn[1, u]))
                for u, point in enumerate(fft(load(other), -1))
            ]
            white = [whiten(a, b) for a, b in zip(fft(load(own), -1), theirs)]
            for z, (re, im) in enumerate(fft(white, 1)):
                spec[z, re_rows, lanes] = re
                spec[z, im_rows, lanes] = im
        return carry

    lax.fori_loop(0, across // 8, meet, 0)

    def edge(held):
        turned = by_left(ah.at[:, :across], al.at[:, :across], held[...])
        turned = by_right(jnp.concatenate((turned[:across], turned[across:]), axis=1), zh, zl)
        return turned[:, :LANES], turned[:, LANES:]

    theirs = times(edge(other_col), (turn_row[0:1, :], turn_row[1:2, :]))
    white = whiten(edge(own_col), theirs)
    back_z = by_right(jnp.concatenate(white, axis=1), bzh, bzl)
    back_z = jnp.concatenate((back_z[:, :LANES], back_z[:, LANES:]), axis=0)
    column[...] = by_left(rh.at[:across], rl.at[:across], back_z)

    surface[...] = jnp.full(surface.shape, -jnp.inf, F32)

    def step(i, carry):
        planes = []
        for n in range(2):
            at = 2 * i + n
            plane = by_left(rh, rl, spec[at])
            middle = jnp.sum(
                jnp.where(lane_is(column.shape, at), column[...], 0.0), axis=1, keepdims=True
            )
            imag0 = plane[across:, :h]
            imag0 = jnp.where(lane_is(imag0.shape, 0), middle, imag0)
            planes.append((plane[:across], imag0, plane[across:, h:]))
        real, imag0, imag = (jnp.concatenate(group, axis=0) for group in zip(*planes))
        z0 = by_right(jnp.concatenate((real[:, :h], imag0), axis=1), b0h, b0l)
        z2 = by_right(jnp.concatenate((real[:, h:q], imag[:, :h]), axis=1), b2h, b2l)
        z1 = by_right(jnp.concatenate((real[:, q:], imag[:, h:]), axis=1), b1h, b1l)
        plus, minus = z0 + z2, z0 - z2
        a, b = z1[:, :q], z1[:, q:]
        for n, part in enumerate((plus + a, minus + b, plus - a, minus - b)):
            lanes = slice(n * q, (n + 1) * q)
            best = jnp.maximum(part[:across], part[across:])
            surface[:, lanes] = jnp.maximum(surface[:, lanes], best)
        return carry

    lax.fori_loop(0, depth // 2, step, 0)


VMEM = pl.BlockSpec(memory_space=pltpu.VMEM)
PARAMS = pltpu.CompilerParams(vmem_limit_bytes=48 * 1024 * 1024)


def whole(shape):
    return pl.BlockSpec(shape, lambda i: (0,) * len(shape))


def spectrum_of(strip, per, forth):
    depth, across, along = strip.shape
    return pl.pallas_call(
        spectrum_kernel,
        grid=(depth // per,),
        out_shape=(
            jax.ShapeDtypeStruct((depth, 2 * across, along // 2), F32),
            jax.ShapeDtypeStruct((across, LANES), F32),
        ),
        in_specs=[pl.BlockSpec((per, across, along), lambda i: (i, 0, 0))]
        + [whole(table.shape) for table in forth[:8]],
        out_specs=(
            pl.BlockSpec((per, 2 * across, along // 2), lambda i: (i, 0, 0)),
            whole((across, LANES)),
        ),
        compiler_params=PARAMS,
        cost_estimate=pl.CostEstimate(
            flops=6 * 10**9, bytes_accessed=10 * 10**6, transcendentals=0
        ),
    )(strip, *forth[:8])


def pair_of(turn, own, other, forth, back):
    depth, rows, half = own[0].shape
    across, along = rows // 2, 2 * half
    row = jnp.pad(turn, ((0, 0), (0, LANES - depth)))
    operands = [own[0], other[0], own[1], other[1], row] + forth[6:10] + back
    return pl.pallas_call(
        pair_kernel,
        out_shape=jax.ShapeDtypeStruct((across, along), F32),
        in_specs=[pl.BlockSpec(memory_space=pltpu.SMEM)] + [VMEM] * len(operands),
        out_specs=VMEM,
        scratch_shapes=[
            pltpu.VMEM((depth, rows, half), F32),
            pltpu.VMEM((across, LANES), F32),
        ],
        compiler_params=PARAMS,
        cost_estimate=pl.CostEstimate(
            flops=12 * 10**9, bytes_accessed=36 * 10**6, transcendentals=0
        ),
    )(turn, *operands)


def on_device(stored, offsets):
    axes = ("tile", "slab")
    slabs = lax.axis_size("slab")
    count = lax.axis_size(axes)
    group = PER_CHIP * slabs
    per, along = stored.shape[1], stored.shape[3]
    depth = per * slabs
    forth, back = make_tables(depth, A, along)
    strides = (1, GC)

    def place_of(t):
        inside = t % group
        return (t // group * PER_CHIP + inside % PER_CHIP) * slabs + inside // PER_CHIP

    def gives(rnd, t):
        to = t - strides[rnd]
        return to >= 0 and (rnd == 1 or to % GC != GC - 1)

    def holder(t, step):
        return t // slabs * slabs + (t - step) % slabs

    near = [(t, t - strides[1 - t % 2]) for t in range(count) if gives(1 - t % 2, t)]
    far = [(t, t - strides[t % 2]) for t in range(count) if gives(t % 2, t)]

    tile, slab = lax.axis_index("tile"), lax.axis_index("slab")
    odd = tile % PER_CHIP
    mine = lax.ppermute(offsets[:, :, 0], axes, [(t, place_of(t)) for t in range(count)])
    bands = []
    for step in range(slabs):
        planes = lax.dynamic_index_in_dim(stored, (slab + step) % slabs, 0, False)
        pairs = [(holder(t, step), place_of(t)) for t in range(count)]
        bands.append(lax.ppermute(planes, axes, pairs))

    def cut(rnd, which):
        return jnp.concatenate(
            [lax.dynamic_slice_in_dim(band, mine[rnd, which], A, 1) for band in bands[::-1]]
        )

    def arrive(strip, pairs):
        return lax.ppermute(strip, axes, [(place_of(t), place_of(to)) for t, to in pairs])

    angles = [phases(np.arange(depth), [per * stride], depth) for stride in strides]
    turns = jnp.asarray(np.stack([[c[:, 0], -s[:, 0]] for c, s in angles]), F32)

    def surface_of(rnd, strip):
        own = spectrum_of(cut(rnd, 0), per, forth)
        turn = lax.dynamic_index_in_dim(turns, rnd, 0, False)
        surface = pair_of(turn, own, spectrum_of(strip, per, forth), forth, back)
        return lax.ppermute(surface, axes, [(place_of(t), t) for t in range(count)])

    given_far, given_near = cut(odd, 1), cut(1 - odd, 1)
    strip_near = arrive(given_near, near)
    strip_far = arrive(given_far, far)
    from_near = surface_of(odd, strip_near)
    from_far = surface_of(1 - odd, strip_far)
    home_odd = (tile * slabs + slab) % 2 == 1
    surface = jnp.stack(
        (jnp.where(home_odd, from_far, from_near), jnp.where(home_odd, from_near, from_far))
    )[:, None]
    return surface, jnp.max(surface, axis=(2, 3))


def solution(mesh):
    return jax.shard_map(
        on_device,
        mesh=mesh,
        in_specs=(P("tile", "slab", None, None), P(None, None, ("tile", "slab"))),
        out_specs=(P(None, ("tile", "slab"), None, None), P(None, ("tile", "slab"))),
        check_vma=False,
    )
```

```python
import math

import jax
import jax.numpy as jnp
import numpy as np
from jax import lax
from jax.experimental import pallas as pl
from jax.experimental.pallas import tpu as pltpu
from jax.sharding import PartitionSpec as P

A = 128
GC = 7
ROUNDS = 2
PER_CHIP = 2
FLOOR = 0.25
LANES = 128
F32 = jnp.float32
BF16 = jnp.bfloat16


def halves(table):
    high = table.astype(np.float32).astype(BF16)
    low = (table - high.astype(np.float64)).astype(np.float32).astype(BF16)
    return jnp.asarray(high), jnp.asarray(low)


def phases(rows, cols, total):
    angle = (np.outer(rows, cols) % total) * (2.0 * math.pi / total)
    return np.cos(angle), np.sin(angle)


def make_tables(depth, across, along):
    quarter = along // 4
    half = quarter // 2
    scale = 1.0 / math.sqrt(depth * across * along)
    at = np.arange(quarter)
    cos0, sin0 = phases(at, 4 * np.arange(half), along)
    sin0 = -sin0
    sin0[:, 0] = np.where(at % 2 == 0, 1.0, -1.0)
    first = np.concatenate((cos0, sin0), axis=1) * scale
    cos2, sin2 = phases(at, 4 * np.arange(half) + 2, along)
    second = np.concatenate((cos2, -sin2), axis=1) * scale
    cos1, sin1 = phases(at, 4 * np.arange(quarter) + 1, along)
    third = np.block([[cos1, -sin1], [-sin1, -cos1]]) * scale
    weight = np.full((2 * half, 1), 2.0)
    weight[0] = weight[half] = 1.0
    cos_a, sin_a = phases(np.arange(across), np.arange(across), across)
    rows = np.block([[cos_a, sin_a], [-sin_a, cos_a]])
    cos_z, sin_z = phases(np.arange(depth), np.arange(depth), depth)
    planes = np.zeros((2 * LANES, 2 * LANES))
    planes[:depth, :depth] = cos_z
    planes[:depth, LANES : LANES + depth] = -sin_z
    planes[LANES : LANES + depth, :depth] = sin_z
    planes[LANES : LANES + depth, LANES : LANES + depth] = cos_z
    forth = [first, second, third, rows, planes]
    back = [first.T * weight, second.T * 2.0, third.T * 2.0, rows.T, planes.T]
    flat = lambda group: [part for table in group for part in halves(table)]
    return flat(forth), flat(back)


def split(x):
    high = x.astype(BF16)
    return high, (x - high.astype(F32)).astype(BF16)


def dot(a, b):
    return jnp.dot(a, b, preferred_element_type=F32)


def by_right(x, high, low):
    xh, xl = split(x)
    return dot(xh, high[...]) + (dot(xl, high[...]) + dot(xh, low[...]))


def by_left(high, low, x):
    xh, xl = split(x)
    return dot(high[...], xh) + (dot(high[...], xl) + dot(low[...], xh))


def fft(points, sign):
    n = len(points)
    if n == 1:
        return points
    even = fft(points[0::2], sign)
    odd = fft(points[1::2], sign)
    out = [None] * n
    for k in range(n // 2):
        re, im = odd[k]
        if k == 0:
            pass
        elif 4 * k == n:
            re, im = (-im, re) if sign > 0 else (im, -re)
        elif 8 * k == n:
            r = math.sqrt(0.5)
            re, im = ((re - im) * r, (im + re) * r) if sign > 0 else ((re + im) * r, (im - re) * r)
        elif 8 * k == 3 * n:
            r = math.sqrt(0.5)
            re, im = ((-re - im) * r, (re - im) * r) if sign > 0 else ((im - re) * r, (-im - re) * r)
        else:
            c = math.cos(2.0 * math.pi * k / n)
            s = sign * math.sin(2.0 * math.pi * k / n)
            re, im = re * c - im * s, im * c + re * s
        out[k] = (even[k][0] + re, even[k][1] + im)
        out[k + n // 2] = (even[k][0] - re, even[k][1] - im)
    return out


def whiten(own, partner):
    re = own[0] * partner[0] + own[1] * partner[1]
    im = own[1] * partner[0] - own[0] * partner[1]
    gain = lax.rsqrt(jnp.maximum(re * re + im * im, FLOOR * FLOOR))
    return re * gain, im * gain


def lane_is(shape, lane):
    return lax.broadcasted_iota(jnp.int32, shape, 1) == lane


def spectrum_kernel(strip, f0h, f0l, f2h, f2l, f1h, f1l, rh, rl, spec, column):
    depth, across, along = strip.shape
    q = along // 4
    h = q // 2
    part = pl.program_id(0)
    x = strip[...].reshape(depth * across, along)
    x0, x1, x2, x3 = (x[:, n * q : (n + 1) * q] for n in range(4))
    s02, s13 = x0 + x2, x1 + x3
    out0 = by_right(s02 + s13, f0h, f0l)
    out2 = by_right(s02 - s13, f2h, f2l)
    out1 = by_right(jnp.concatenate((x0 - x2, x1 - x3), axis=1), f1h, f1l)
    imag0 = out0[:, h:]
    first = lane_is(imag0.shape, 0)
    real = jnp.concatenate((out0[:, :h], out2[:, :h], out1[:, :q]), axis=1)
    imag = jnp.concatenate((jnp.where(first, 0.0, imag0), out2[:, h:], out1[:, q:]), axis=1)
    middles = jnp.where(part == 0, 0.0, column[...])
    for n in range(depth):
        rows = slice(n * across, (n + 1) * across)
        spec[n] = by_left(rh, rl, jnp.concatenate((real[rows], imag[rows]), axis=0))
        middle = jnp.broadcast_to(imag0[rows, 0:1], column.shape)
        middles = jnp.where(lane_is(column.shape, part * depth + n), middle, middles)
    column[...] = middles


def pair_kernel(own, other, own_col, other_col, *refs):
    (ah, al, zh, zl), back = refs[:4], refs[4:14]
    surface, spec, column = refs[14:]
    b0h, b0l, b2h, b2l, b1h, b1l, rh, rl, bzh, bzl = back
    depth = own.shape[0]
    across, along = surface.shape
    q = along // 4
    h = q // 2

    def meet(i, carry):
        re_rows = pl.ds(pl.multiple_of(8 * i, 8), 8)
        im_rows = pl.ds(pl.multiple_of(across + 8 * i, 8), 8)
        for lane in range(0, along // 2, LANES):
            lanes = slice(lane, lane + LANES)
            load = lambda held: [(held[z, re_rows, lanes], held[z, im_rows, lanes]) for z in range(depth)]
            white = [whiten(a, b) for a, b in zip(fft(load(own), -1), fft(load(other), -1))]
            for z, (re, im) in enumerate(fft(white, 1)):
                spec[z, re_rows, lanes] = re
                spec[z, im_rows, lanes] = im
        return carry

    lax.fori_loop(0, across // 8, meet, 0)

    def edge(held):
        turned = by_left(ah.at[:, :across], al.at[:, :across], held[...])
        turned = by_right(jnp.concatenate((turned[:across], turned[across:]), axis=1), zh, zl)
        return turned[:, :LANES], turned[:, LANES:]

    white = whiten(edge(own_col), edge(other_col))
    back_z = by_right(jnp.concatenate(white, axis=1), bzh, bzl)
    back_z = jnp.concatenate((back_z[:, :LANES], back_z[:, LANES:]), axis=0)
    column[...] = by_left(rh.at[:across], rl.at[:across], back_z)

    surface[...] = jnp.full(surface.shape, -jnp.inf, F32)

    def step(i, carry):
        planes = []
        for n in range(2):
            at = 2 * i + n
            plane = by_left(rh, rl, spec[at])
            middle = jnp.sum(
                jnp.where(lane_is(column.shape, at), column[...], 0.0), axis=1, keepdims=True
            )
            imag0 = plane[across:, :h]
            imag0 = jnp.where(lane_is(imag0.shape, 0), middle, imag0)
            planes.append((plane[:across], imag0, plane[across:, h:]))
        real, imag0, imag = (jnp.concatenate(group, axis=0) for group in zip(*planes))
        z0 = by_right(jnp.concatenate((real[:, :h], imag0), axis=1), b0h, b0l)
        z2 = by_right(jnp.concatenate((real[:, h:q], imag[:, :h]), axis=1), b2h, b2l)
        z1 = by_right(jnp.concatenate((real[:, q:], imag[:, h:]), axis=1), b1h, b1l)
        plus, minus = z0 + z2, z0 - z2
        a, b = z1[:, :q], z1[:, q:]
        for n, part in enumerate((plus + a, minus + b, plus - a, minus - b)):
            lanes = slice(n * q, (n + 1) * q)
            best = jnp.maximum(part[:across], part[across:])
            surface[:, lanes] = jnp.maximum(surface[:, lanes], best)
        return carry

    lax.fori_loop(0, depth // 2, step, 0)


VMEM = pl.BlockSpec(memory_space=pltpu.VMEM)
PARAMS = pltpu.CompilerParams(vmem_limit_bytes=48 * 1024 * 1024)


def whole(shape):
    return pl.BlockSpec(shape, lambda i: (0,) * len(shape))


def spectrum_of(strip, per, forth):
    depth, across, along = strip.shape
    return pl.pallas_call(
        spectrum_kernel,
        grid=(depth // per,),
        out_shape=(
            jax.ShapeDtypeStruct((depth, 2 * across, along // 2), F32),
            jax.ShapeDtypeStruct((across, LANES), F32),
        ),
        in_specs=[pl.BlockSpec((per, across, along), lambda i: (i, 0, 0))]
        + [whole(table.shape) for table in forth[:8]],
        out_specs=(
            pl.BlockSpec((per, 2 * across, along // 2), lambda i: (i, 0, 0)),
            whole((across, LANES)),
        ),
        compiler_params=PARAMS,
        cost_estimate=pl.CostEstimate(
            flops=6 * 10**9, bytes_accessed=10 * 10**6, transcendentals=0
        ),
    )(strip, *forth[:8])


def pair_of(own, other, forth, back):
    depth, rows, half = own[0].shape
    across, along = rows // 2, 2 * half
    operands = [own[0], other[0], own[1], other[1]] + forth[6:10] + back
    return pl.pallas_call(
        pair_kernel,
        out_shape=jax.ShapeDtypeStruct((across, along), F32),
        in_specs=[VMEM] * len(operands),
        out_specs=VMEM,
        scratch_shapes=[
            pltpu.VMEM((depth, rows, half), F32),
            pltpu.VMEM((across, LANES), F32),
        ],
        compiler_params=PARAMS,
        cost_estimate=pl.CostEstimate(
            flops=12 * 10**9, bytes_accessed=36 * 10**6, transcendentals=0
        ),
    )(*operands)


def work_place(t, slabs):
    inside = t % (PER_CHIP * slabs)
    return t // (PER_CHIP * slabs) * PER_CHIP + inside % PER_CHIP, inside // PER_CHIP


def exchange_kernel(slabs, stored, band, send_sems, recv_sems, local_sem):
    tile, slab = lax.axis_index("tile"), lax.axis_index("slab")
    here = tile // PER_CHIP * PER_CHIP * slabs + slab * PER_CHIP + tile % PER_CHIP
    home = here // slabs
    stays = home == tile
    barrier = pltpu.get_barrier_semaphore()

    def signal(j):
        pl.semaphore_signal(
            barrier, inc=1, device_id=(home, j), device_id_type=pl.DeviceIdType.MESH
        )

    for j in range(slabs):
        pl.when(jnp.logical_not(jnp.logical_and(stays, slab == j)))(lambda j=j: signal(j))
    pl.semaphore_wait(barrier, slabs - stays.astype(jnp.int32))

    local = pltpu.make_async_copy(stored.at[here % slabs], band.at[slab], local_sem)
    pl.when(stays)(local.start)
    copies = []
    for step in range(slabs):
        inside = (slab + step) % slabs
        to = work_place(tile * slabs + inside, slabs)
        copy = pltpu.make_async_remote_copy(
            src_ref=stored.at[inside],
            dst_ref=band.at[slab],
            send_sem=send_sems.at[step],
            recv_sem=recv_sems.at[slab],
            device_id=to,
            device_id_type=pl.DeviceIdType.MESH,
        )
        away = jnp.logical_not(jnp.logical_and(to[0] == tile, to[1] == slab))
        pl.when(away)(copy.start)
        copies.append((away, copy))
    for away, copy in copies:
        pl.when(away)(copy.wait_send)
    for j in range(slabs):
        arriving = pltpu.make_async_remote_copy(
            src_ref=stored.at[0],
            dst_ref=band.at[j],
            send_sem=send_sems.at[0],
            recv_sem=recv_sems.at[j],
            device_id=(home, j),
            device_id_type=pl.DeviceIdType.MESH,
        )
        pl.when(jnp.logical_not(jnp.logical_and(stays, slab == j)))(arriving.wait_recv)
    pl.when(stays)(local.wait)


def exchange(stored):
    slabs = lax.axis_size("slab")
    _, per, rows, along = stored.shape
    band = pl.pallas_call(
        lambda *refs: exchange_kernel(slabs, *refs),
        out_shape=jax.ShapeDtypeStruct((slabs, per, rows, along), F32),
        in_specs=[pl.BlockSpec(memory_space=pl.ANY)],
        out_specs=pl.BlockSpec(memory_space=pl.ANY),
        scratch_shapes=[
            pltpu.SemaphoreType.DMA((slabs,)),
            pltpu.SemaphoreType.DMA((slabs,)),
            pltpu.SemaphoreType.DMA,
        ],
        compiler_params=pltpu.CompilerParams(
            collective_id=0, has_side_effects=True, vmem_limit_bytes=48 * 1024 * 1024
        ),
        cost_estimate=pl.CostEstimate(
            flops=0, bytes_accessed=2 * stored.size * 4, transcendentals=0
        ),
    )(stored)
    return band.reshape(slabs * per, rows, along)


def on_device(stored, offsets):
    axes = ("tile", "slab")
    slabs = lax.axis_size("slab")
    count = lax.axis_size(axes)
    per, along = stored.shape[1], stored.shape[3]
    forth, back = make_tables(per * slabs, A, along)
    strides = (1, GC)

    def place_of(t):
        to = work_place(t, slabs)
        return to[0] * slabs + to[1]

    def gives(rnd, t):
        to = t - strides[rnd]
        return to >= 0 and (rnd == 1 or to % GC != GC - 1)

    near = [(t, t - strides[1 - t % 2]) for t in range(count) if gives(1 - t % 2, t)]
    far = [(t, t - strides[t % 2]) for t in range(count) if gives(t % 2, t)]

    tile, slab = lax.axis_index("tile"), lax.axis_index("slab")
    odd = tile % PER_CHIP
    mine = lax.ppermute(offsets[:, :, 0], axes, [(t, place_of(t)) for t in range(count)])
    band = exchange(stored)

    def cut(rnd, which):
        return lax.dynamic_slice_in_dim(band, mine[rnd, which], A, 1)

    def arrive(strip, pairs):
        return lax.ppermute(strip, axes, [(place_of(t), place_of(to)) for t, to in pairs])

    def surface_of(rnd, strip):
        own = spectrum_of(cut(rnd, 0), per, forth)
        surface = pair_of(own, spectrum_of(strip, per, forth), forth, back)
        return lax.ppermute(surface, axes, [(place_of(t), t) for t in range(count)])

    given_far, given_near = cut(odd, 1), cut(1 - odd, 1)
    strip_far = arrive(given_far, far)
    strip_near = arrive(given_near, near)
    from_near = surface_of(odd, strip_near)
    from_far = surface_of(1 - odd, strip_far)
    home_odd = (tile * slabs + slab) % 2 == 1
    surface = jnp.stack(
        (jnp.where(home_odd, from_far, from_near), jnp.where(home_odd, from_near, from_far))
    )[:, None]
    return surface, jnp.max(surface, axis=(2, 3))


def solution(mesh):
    return jax.shard_map(
        on_device,
        mesh=mesh,
        in_specs=(P("tile", "slab", None, None), P(None, None, ("tile", "slab"))),
        out_specs=(P(None, ("tile", "slab"), None, None), P(None, ("tile", "slab"))),
        check_vma=False,
    )
```

```python
import math

import jax
import jax.numpy as jnp
import numpy as np
from jax import lax
from jax.experimental import pallas as pl
from jax.experimental.pallas import tpu as pltpu
from jax.sharding import PartitionSpec as P

A = 128
GC = 7
ROUNDS = 2
PER_CHIP = 2
FLOOR = 0.25
LANES = 128
F32 = jnp.float32
BF16 = jnp.bfloat16


def halves(table):
    high = table.astype(np.float32).astype(BF16)
    low = (table - high.astype(np.float64)).astype(np.float32).astype(BF16)
    return jnp.asarray(high), jnp.asarray(low)


def phases(rows, cols, total):
    angle = (np.outer(rows, cols) % total) * (2.0 * math.pi / total)
    return np.cos(angle), np.sin(angle)


def make_tables(depth, across, along):
    quarter = along // 4
    half = quarter // 2
    scale = 1.0 / math.sqrt(depth * across * along)
    at = np.arange(quarter)
    cos0, sin0 = phases(at, 4 * np.arange(half), along)
    sin0 = -sin0
    sin0[:, 0] = np.where(at % 2 == 0, 1.0, -1.0)
    first = np.concatenate((cos0, sin0), axis=1) * scale
    cos2, sin2 = phases(at, 4 * np.arange(half) + 2, along)
    second = np.concatenate((cos2, -sin2), axis=1) * scale
    cos1, sin1 = phases(at, 4 * np.arange(quarter) + 1, along)
    third = np.block([[cos1, -sin1], [-sin1, -cos1]]) * scale
    weight = np.full((2 * half, 1), 2.0)
    weight[0] = weight[half] = 1.0
    cos_a, sin_a = phases(np.arange(across), np.arange(across), across)
    rows = np.block([[cos_a, sin_a], [-sin_a, cos_a]])
    cos_z, sin_z = phases(np.arange(depth), np.arange(depth), depth)
    planes = np.zeros((2 * LANES, 2 * LANES))
    planes[:depth, :depth] = cos_z
    planes[:depth, LANES : LANES + depth] = -sin_z
    planes[LANES : LANES + depth, :depth] = sin_z
    planes[LANES : LANES + depth, LANES : LANES + depth] = cos_z
    forth = [first, second, third, rows, planes]
    back = [first.T * weight, second.T * 2.0, third.T * 2.0, rows.T, planes.T]
    flat = lambda group: [part for table in group for part in halves(table)]
    return flat(forth), flat(back)


def split(x):
    high = x.astype(BF16)
    return high, (x - high.astype(F32)).astype(BF16)


def dot(a, b):
    return jnp.dot(a, b, preferred_element_type=F32)


def by_right(x, high, low):
    xh, xl = split(x)
    return dot(xh, high[...]) + (dot(xl, high[...]) + dot(xh, low[...]))


def by_left(high, low, x):
    xh, xl = split(x)
    return dot(high[...], xh) + (dot(high[...], xl) + dot(low[...], xh))


def fft(points, sign):
    n = len(points)
    if n == 1:
        return points
    even = fft(points[0::2], sign)
    odd = fft(points[1::2], sign)
    out = [None] * n
    for k in range(n // 2):
        re, im = odd[k]
        if k == 0:
            pass
        elif 4 * k == n:
            re, im = (-im, re) if sign > 0 else (im, -re)
        elif 8 * k == n:
            r = math.sqrt(0.5)
            re, im = ((re - im) * r, (im + re) * r) if sign > 0 else ((re + im) * r, (im - re) * r)
        elif 8 * k == 3 * n:
            r = math.sqrt(0.5)
            re, im = ((-re - im) * r, (re - im) * r) if sign > 0 else ((im - re) * r, (-im - re) * r)
        else:
            c = math.cos(2.0 * math.pi * k / n)
            s = sign * math.sin(2.0 * math.pi * k / n)
            re, im = re * c - im * s, im * c + re * s
        out[k] = (even[k][0] + re, even[k][1] + im)
        out[k + n // 2] = (even[k][0] - re, even[k][1] - im)
    return out


def whiten(own, partner):
    re = own[0] * partner[0] + own[1] * partner[1]
    im = own[1] * partner[0] - own[0] * partner[1]
    gain = lax.rsqrt(jnp.maximum(re * re + im * im, FLOOR * FLOOR))
    return re * gain, im * gain


def lane_is(shape, lane):
    return lax.broadcasted_iota(jnp.int32, shape, 1) == lane


def spectrum_kernel(strip, f0h, f0l, f2h, f2l, f1h, f1l, rh, rl, spec, column):
    depth, across, along = strip.shape
    q = along // 4
    h = q // 2
    part = pl.program_id(0)
    x = strip[...].reshape(depth * across, along)
    x0, x1, x2, x3 = (x[:, n * q : (n + 1) * q] for n in range(4))
    s02, s13 = x0 + x2, x1 + x3
    out0 = by_right(s02 + s13, f0h, f0l)
    out2 = by_right(s02 - s13, f2h, f2l)
    out1 = by_right(jnp.concatenate((x0 - x2, x1 - x3), axis=1), f1h, f1l)
    imag0 = out0[:, h:]
    first = lane_is(imag0.shape, 0)
    real = jnp.concatenate((out0[:, :h], out2[:, :h], out1[:, :q]), axis=1)
    imag = jnp.concatenate((jnp.where(first, 0.0, imag0), out2[:, h:], out1[:, q:]), axis=1)
    middles = jnp.where(part == 0, 0.0, column[...])
    for n in range(depth):
        rows = slice(n * across, (n + 1) * across)
        spec[n] = by_left(rh, rl, jnp.concatenate((real[rows], imag[rows]), axis=0))
        middle = jnp.broadcast_to(imag0[rows, 0:1], column.shape)
        middles = jnp.where(lane_is(column.shape, part * depth + n), middle, middles)
    column[...] = middles


def pair_kernel(own, other, own_col, other_col, *refs):
    (ah, al, zh, zl), back = refs[:4], refs[4:14]
    surface, spec, column = refs[14:]
    b0h, b0l, b2h, b2l, b1h, b1l, rh, rl, bzh, bzl = back
    depth = own.shape[0]
    across, along = surface.shape
    q = along // 4
    h = q // 2

    def meet(i, carry):
        re_rows = pl.ds(pl.multiple_of(8 * i, 8), 8)
        im_rows = pl.ds(pl.multiple_of(across + 8 * i, 8), 8)
        for lane in range(0, along // 2, LANES):
            lanes = slice(lane, lane + LANES)
            load = lambda held: [(held[z, re_rows, lanes], held[z, im_rows, lanes]) for z in range(depth)]
            white = [whiten(a, b) for a, b in zip(fft(load(own), -1), fft(load(other), -1))]
            for z, (re, im) in enumerate(fft(white, 1)):
                spec[z, re_rows, lanes] = re
                spec[z, im_rows, lanes] = im
        return carry

    lax.fori_loop(0, across // 8, meet, 0)

    def edge(held):
        turned = by_left(ah.at[:, :across], al.at[:, :across], held[...])
        turned = by_right(jnp.concatenate((turned[:across], turned[across:]), axis=1), zh, zl)
        return turned[:, :LANES], turned[:, LANES:]

    white = whiten(edge(own_col), edge(other_col))
    back_z = by_right(jnp.concatenate(white, axis=1), bzh, bzl)
    back_z = jnp.concatenate((back_z[:, :LANES], back_z[:, LANES:]), axis=0)
    column[...] = by_left(rh.at[:across], rl.at[:across], back_z)

    surface[...] = jnp.full(surface.shape, -jnp.inf, F32)

    def step(i, carry):
        planes = []
        for n in range(2):
            at = 2 * i + n
            plane = by_left(rh, rl, spec[at])
            middle = jnp.sum(
                jnp.where(lane_is(column.shape, at), column[...], 0.0), axis=1, keepdims=True
            )
            imag0 = plane[across:, :h]
            imag0 = jnp.where(lane_is(imag0.shape, 0), middle, imag0)
            planes.append((plane[:across], imag0, plane[across:, h:]))
        real, imag0, imag = (jnp.concatenate(group, axis=0) for group in zip(*planes))
        z0 = by_right(jnp.concatenate((real[:, :h], imag0), axis=1), b0h, b0l)
        z2 = by_right(jnp.concatenate((real[:, h:q], imag[:, :h]), axis=1), b2h, b2l)
        z1 = by_right(jnp.concatenate((real[:, q:], imag[:, h:]), axis=1), b1h, b1l)
        plus, minus = z0 + z2, z0 - z2
        a, b = z1[:, :q], z1[:, q:]
        for n, part in enumerate((plus + a, minus + b, plus - a, minus - b)):
            lanes = slice(n * q, (n + 1) * q)
            best = jnp.maximum(part[:across], part[across:])
            surface[:, lanes] = jnp.maximum(surface[:, lanes], best)
        return carry

    lax.fori_loop(0, depth // 2, step, 0)


VMEM = pl.BlockSpec(memory_space=pltpu.VMEM)
PARAMS = pltpu.CompilerParams(vmem_limit_bytes=48 * 1024 * 1024)


def whole(shape):
    return pl.BlockSpec(shape, lambda i: (0,) * len(shape))


def spectrum_of(strip, per, forth):
    depth, across, along = strip.shape
    return pl.pallas_call(
        spectrum_kernel,
        grid=(depth // per,),
        out_shape=(
            jax.ShapeDtypeStruct((depth, 2 * across, along // 2), F32),
            jax.ShapeDtypeStruct((across, LANES), F32),
        ),
        in_specs=[pl.BlockSpec((per, across, along), lambda i: (i, 0, 0))]
        + [whole(table.shape) for table in forth[:8]],
        out_specs=(
            pl.BlockSpec((per, 2 * across, along // 2), lambda i: (i, 0, 0)),
            whole((across, LANES)),
        ),
        compiler_params=PARAMS,
        cost_estimate=pl.CostEstimate(
            flops=6 * 10**9, bytes_accessed=10 * 10**6, transcendentals=0
        ),
    )(strip, *forth[:8])


def pair_of(own, other, forth, back):
    depth, rows, half = own[0].shape
    across, along = rows // 2, 2 * half
    operands = [own[0], other[0], own[1], other[1]] + forth[6:10] + back
    return pl.pallas_call(
        pair_kernel,
        out_shape=jax.ShapeDtypeStruct((across, along), F32),
        in_specs=[VMEM] * len(operands),
        out_specs=VMEM,
        scratch_shapes=[
            pltpu.VMEM((depth, rows, half), F32),
            pltpu.VMEM((across, LANES), F32),
        ],
        compiler_params=PARAMS,
        cost_estimate=pl.CostEstimate(
            flops=12 * 10**9, bytes_accessed=36 * 10**6, transcendentals=0
        ),
    )(*operands)


def work_place(t, slabs):
    inside = t % (PER_CHIP * slabs)
    return t // (PER_CHIP * slabs) * PER_CHIP + inside % PER_CHIP, inside // PER_CHIP


def exchange_kernel(slabs, stored, band, send_sems, recv_sems, local_sem):
    tile, slab = lax.axis_index("tile"), lax.axis_index("slab")
    here = tile // PER_CHIP * PER_CHIP * slabs + slab * PER_CHIP + tile % PER_CHIP
    home = here // slabs
    stays = home == tile
    barrier = pltpu.get_barrier_semaphore()

    def signal(j):
        pl.semaphore_signal(
            barrier, inc=1, device_id=(home, j), device_id_type=pl.DeviceIdType.MESH
        )

    for j in range(slabs):
        pl.when(jnp.logical_not(jnp.logical_and(stays, slab == j)))(lambda j=j: signal(j))
    pl.semaphore_wait(barrier, slabs - stays.astype(jnp.int32))

    local = pltpu.make_async_copy(stored.at[here % slabs], band.at[slab], local_sem)
    pl.when(stays)(local.start)
    copies = []
    for step in range(slabs):
        inside = (slab + step) % slabs
        to = work_place(tile * slabs + inside, slabs)
        copy = pltpu.make_async_remote_copy(
            src_ref=stored.at[inside],
            dst_ref=band.at[slab],
            send_sem=send_sems.at[step],
            recv_sem=recv_sems.at[slab],
            device_id=to,
            device_id_type=pl.DeviceIdType.MESH,
        )
        away = jnp.logical_not(jnp.logical_and(to[0] == tile, to[1] == slab))
        pl.when(away)(copy.start)
        copies.append((away, copy))
    for away, copy in copies:
        pl.when(away)(copy.wait_send)
    for j in range(slabs):
        arriving = pltpu.make_async_remote_copy(
            src_ref=stored.at[0],
            dst_ref=band.at[j],
            send_sem=send_sems.at[0],
            recv_sem=recv_sems.at[j],
            device_id=(home, j),
            device_id_type=pl.DeviceIdType.MESH,
        )
        pl.when(jnp.logical_not(jnp.logical_and(stays, slab == j)))(arriving.wait_recv)
    pl.when(stays)(local.wait)


def exchange(stored):
    slabs = lax.axis_size("slab")
    _, per, rows, along = stored.shape
    band = pl.pallas_call(
        lambda *refs: exchange_kernel(slabs, *refs),
        out_shape=jax.ShapeDtypeStruct((slabs, per, rows, along), F32),
        in_specs=[pl.BlockSpec(memory_space=pl.ANY)],
        out_specs=pl.BlockSpec(memory_space=pl.ANY),
        scratch_shapes=[
            pltpu.SemaphoreType.DMA((slabs,)),
            pltpu.SemaphoreType.DMA((slabs,)),
            pltpu.SemaphoreType.DMA,
        ],
        compiler_params=pltpu.CompilerParams(
            collective_id=0, has_side_effects=True, vmem_limit_bytes=48 * 1024 * 1024
        ),
        cost_estimate=pl.CostEstimate(
            flops=0, bytes_accessed=2 * stored.size * 4, transcendentals=0
        ),
    )(stored)
    return band.reshape(slabs * per, rows, along)


def on_device(stored, offsets):
    axes = ("tile", "slab")
    slabs = lax.axis_size("slab")
    count = lax.axis_size(axes)
    per, along = stored.shape[1], stored.shape[3]
    forth, back = make_tables(per * slabs, A, along)
    strides = (1, GC)

    def place_of(t):
        to = work_place(t, slabs)
        return to[0] * slabs + to[1]

    def gives(rnd, t):
        to = t - strides[rnd]
        return to >= 0 and (rnd == 1 or to % GC != GC - 1)

    near = [(t, t - strides[1 - t % 2]) for t in range(count) if gives(1 - t % 2, t)]
    far = [(t, t - strides[t % 2]) for t in range(count) if gives(t % 2, t)]

    tile, slab = lax.axis_index("tile"), lax.axis_index("slab")
    odd = tile % PER_CHIP
    mine = lax.ppermute(offsets[:, :, 0], axes, [(t, place_of(t)) for t in range(count)])
    band = exchange(stored)

    def cut(planes, rnd, which):
        return lax.dynamic_slice_in_dim(planes, mine[rnd, which], A, 1)

    def arrive(strip, pairs):
        return lax.ppermute(strip, axes, [(place_of(t), place_of(to)) for t, to in pairs])

    def send_home(surface):
        return lax.ppermute(surface, axes, [(place_of(t), t) for t in range(count)])

    given_far, given_near = cut(band, odd, 1), cut(band, 1 - odd, 1)
    band, given_far, given_near = lax.optimization_barrier((band, given_far, given_near))
    strip_far = arrive(given_far, far)
    strip_near = arrive(given_near, near)
    own_near = spectrum_of(cut(band, odd, 0), per, forth)
    own_far = spectrum_of(cut(band, 1 - odd, 0), per, forth)
    surface_near = pair_of(own_near, spectrum_of(strip_near, per, forth), forth, back)
    from_near = send_home(surface_near)
    strip_far, _ = lax.optimization_barrier((strip_far, surface_near))
    surface_far = pair_of(own_far, spectrum_of(strip_far, per, forth), forth, back)
    from_far = send_home(surface_far)
    home_odd = (tile * slabs + slab) % 2 == 1
    surface = jnp.stack(
        (jnp.where(home_odd, from_far, from_near), jnp.where(home_odd, from_near, from_far))
    )[:, None]
    return surface, jnp.max(surface, axis=(2, 3))


def solution(mesh):
    return jax.shard_map(
        on_device,
        mesh=mesh,
        in_specs=(P("tile", "slab", None, None), P(None, None, ("tile", "slab"))),
        out_specs=(P(None, ("tile", "slab"), None, None), P(None, ("tile", "slab"))),
        check_vma=False,
    )
```
